32 devices in a mesh: rows: 8 (over z, y), feat: 4 (over x, core).
Axes of the slice: x: 2, y: 2, z: 4, core: 2. Of those that a mesh axis runs over, the one named last changes fastest.
Arguments:
- node_feats: float32 [256, 8192], P('feat', 'rows'), may hold values from -6 to 6
- theta: float32 [256, 256], P(None, 'feat'), may hold values from -0.375 to 0.375
- cotangent: float32 [256, 8192], P('feat', 'rows'), may hold values from -6 to 6
- remote_mol: int32 [64, 2], P('rows'), may hold values from 0 to 15
- remote_rxn: int32 [64, 2], P('rows'), may hold values from 0 to 15
- remote_count: int32 [64], P('rows'), may hold values from 0 to 2, as said below
- remote_tiles: int32 [64, 2, 4096], P('rows'), may hold values 0 or 1
- local_mol: int32 [256], P('rows'), may hold values from 0 to 15
- local_rxn: int32 [256], P('rows'), may hold values from 0 to 15
- local_tiles: int32 [256, 4096], P('rows'), may hold values 0 or 1
Outputs:
- out_feats: float32 [256, 8192], P('feat', 'rows')
- theta_grad: float32 [256, 256], P(None, 'feat')
The draws below stay inside these ranges and needn't reach their ends.
Inputs may be any that keep to these rules, and one draw needn't show every extreme that they name: `remote_count`: for each source index, the live slots to each destination; one destination is filled to 2 from every source.
All inputs are finite; a program needn't handle non-finite values. No bound on the sum of `remote_tiles` or of `local_tiles` on one device may be relied on, other than what follows from the above.
Results may differ from the reference program's by a relative error of at most 0.0001.
Values sent between devices are 32-bit elements; how exact they have to be, the bound alone decides.
A program may use at most 128 MiB of HBM per device.

```python
import jax
import jax.numpy as jnp
from jax import lax

F = 256
BLK = 64
MB_DEV = 16
RB_DEV = 16
LOC_DEV = 32
CAP = 2
MOLS = 8192
PAIRS = 64
LOCAL = 256
N_ROWS = 8


def draw_remote_count(key, part):
    first = jax.random.fold_in(key, 11)
    second = jax.random.fold_in(key, 23)
    base = jax.random.randint(first, (N_ROWS, N_ROWS), 0, CAP + 1)
    hottest = jax.random.randint(second, (), 0, N_ROWS)
    column = jnp.arange(N_ROWS, dtype=jnp.int32)[None, :]
    base = jnp.where(column == hottest, CAP, base)
    return base.reshape(N_ROWS * N_ROWS).astype(jnp.int32)


def with_ends(array, stream_key, least, largest):
    extent = array.shape
    place = [jax.random.randint(jax.random.fold_in(stream_key, axis), (), 0, extent[axis]) for axis in range(len(extent))]
    array = array.at[tuple(place)].set(least)
    longest = extent.index(max(extent))
    place[longest] = (place[longest] + 1) % extent[longest]
    return array.at[tuple(place)].set(largest)


def block_levels(own_key, shape, split, least, high):
    loudness, own = 1.0, jax.random.fold_in(own_key, 6)
    for position, shards_of in split:
        heights = jnp.exp(jax.random.uniform(jax.random.fold_in(own, position), (shards_of,), jnp.float32, least / len(split), high / len(split)))
        loudness = loudness * jnp.repeat(heights, shape[position] // shards_of).reshape([-1 if axis == position else 1 for axis in range(len(shape))])
    return loudness


def scatter_about(stream_key, extent, spread, most, shards=(), kind=jnp.bfloat16):
    array = spread * jax.random.normal(stream_key, extent, jnp.float32)
    if shards:
        array = array * block_levels(stream_key, extent, shards, -0.22, 0.18)
    return jnp.clip(array, -most, most).astype(kind)


def setup_inputs(seed: int = 0) -> dict:
    seeds = jax.random.split(jax.random.key(seed), 11)
    return {
        "node_feats": scatter_about(seeds[0], (F, MOLS), 1.0, 6.0, ((0, 4), (1, 8)), jnp.float32),
        "theta": scatter_about(seeds[1], (F, F), F ** -0.5, 0.375, ((1, 4),), jnp.float32),
        "cotangent": scatter_about(seeds[2], (F, MOLS), 1.0, 6.0, ((0, 4), (1, 8)), jnp.float32),
        "remote_mol": with_ends(jax.random.randint(seeds[3], (PAIRS, CAP), 0, MB_DEV), jax.random.fold_in(seeds[3], 1), 0, MB_DEV - 1).astype(jnp.int32),
        "remote_rxn": with_ends(jax.random.randint(seeds[4], (PAIRS, CAP), 0, RB_DEV), jax.random.fold_in(seeds[4], 1), 0, RB_DEV - 1).astype(jnp.int32),
        "remote_count": draw_remote_count(jax.random.fold_in(seeds[10], 71), 0),
        "remote_tiles": with_ends((jax.random.randint(seeds[6], (PAIRS, CAP, BLK * BLK), 0, min(32, BLK // 2)) < 1).astype(jnp.int32), jax.random.fold_in(seeds[6], 1), 0, 1),
        "local_mol": with_ends(jax.random.randint(seeds[7], (LOCAL,), 0, MB_DEV), jax.random.fold_in(seeds[7], 1), 0, MB_DEV - 1).astype(jnp.int32),
        "local_rxn": with_ends(jax.random.randint(seeds[8], (LOCAL,), 0, RB_DEV), jax.random.fold_in(seeds[8], 1), 0, RB_DEV - 1).astype(jnp.int32),
        "local_tiles": with_ends((jax.random.randint(seeds[9], (LOCAL, BLK * BLK), 0, min(32, BLK // 2)) < 1).astype(jnp.int32), jax.random.fold_in(seeds[9], 1), 0, 1),
    }


def block_lists(remote_mol, remote_rxn, remote_count, local_mol, local_rxn):
    pair = jnp.arange(N_ROWS * N_ROWS, dtype=jnp.int32)
    source = pair // N_ROWS
    target = pair % N_ROWS
    rmol = (source[:, None] * MB_DEV + remote_mol).astype(jnp.int32).reshape(N_ROWS, N_ROWS * CAP)
    rrxn = (target[:, None] * RB_DEV + remote_rxn).astype(jnp.int32).reshape(N_ROWS, N_ROWS * CAP)
    live = (jnp.arange(CAP, dtype=jnp.int32)[None, :] < remote_count[:, None]).reshape(N_ROWS, N_ROWS * CAP)
    lsrc = jnp.arange(N_ROWS * LOC_DEV, dtype=jnp.int32) // LOC_DEV
    lmol = (lsrc * MB_DEV + local_mol).astype(jnp.int32).reshape(N_ROWS, LOC_DEV)
    lrxn = (lsrc * RB_DEV + local_rxn).astype(jnp.int32).reshape(N_ROWS, LOC_DEV)
    return (rmol, rrxn, live, lmol, lrxn)

def step_tiles(rtile, live, ltile):
    rt = rtile.astype(jnp.float32).reshape(N_ROWS * CAP, BLK, BLK) * live.astype(jnp.float32)[:, None, None]
    lt = ltile.astype(jnp.float32).reshape(LOC_DEV, BLK, BLK)
    return jnp.concatenate([rt, lt], axis=0)

def reference(node_feats, theta, cotangent, remote_mol, remote_rxn, remote_count, remote_tiles, local_mol, local_rxn, local_tiles):
    rmol, rrxn, live, lmol, lrxn = block_lists(remote_mol, remote_rxn, remote_count, local_mol, local_rxn)
    rtiles = remote_tiles.reshape(N_ROWS, N_ROWS * CAP, BLK * BLK)
    ltiles = local_tiles.reshape(N_ROWS, LOC_DEV, BLK * BLK)
    mol_all = jnp.concatenate([rmol, lmol], axis=1)
    rxn_all = jnp.concatenate([rrxn, lrxn], axis=1)
    total_mb = MB_DEV * N_ROWS
    total_rb = RB_DEV * N_ROWS
    xs = (rtiles, live, ltiles, mol_all, rxn_all)

    def degree_step(carry, item):
        vdeg, edeg = carry
        rt, lv, lt, mol, rxn = item
        tiles = step_tiles(rt, lv, lt)
        vdeg = vdeg.at[mol].add(lax.optimization_barrier(jnp.sum(tiles, axis=2)))
        edeg = edeg.at[rxn].add(lax.optimization_barrier(jnp.sum(tiles, axis=1)))
        return ((vdeg, edeg), None)
    zero_v = jnp.ones((total_mb, BLK), jnp.float32)
    zero_e = jnp.ones((total_rb, BLK), jnp.float32)
    (vdeg, edeg), _ = lax.scan(degree_step, (zero_v, zero_e), xs)
    vscale = 1.0 / jnp.sqrt(vdeg)

    def propagate(values):
        width = values.shape[1]
        vb = values.reshape(total_mb, BLK, width) * vscale[:, :, None]

        def forward_step(acc, item):
            rt, lv, lt, mol, rxn = item
            tiles = step_tiles(rt, lv, lt)
            part = jnp.einsum('kij,kif->kjf', tiles, vb[mol], precision=lax.Precision.HIGHEST)
            return (acc.at[rxn].add(part), None)
        acc, _ = lax.scan(forward_step, jnp.zeros((total_rb, BLK, width), jnp.float32), xs)
        edge = acc / edeg[:, :, None]

        def back_step(acc, item):
            rt, lv, lt, mol, rxn = item
            tiles = step_tiles(rt, lv, lt)
            part = jnp.einsum('kij,kjf->kif', tiles, edge[rxn], precision=lax.Precision.HIGHEST)
            return (acc.at[mol].add(part), None)
        accm, _ = lax.scan(back_step, jnp.zeros((total_mb, BLK, width), jnp.float32), xs)
        return (accm * vscale[:, :, None]).reshape(total_mb * BLK, width)
    feats = node_feats.T
    grads = cotangent.T
    hidden = jnp.dot(feats, theta, precision=lax.Precision.HIGHEST)
    mixed = propagate(hidden)
    output = jnp.tanh(mixed)
    grad_mixed = grads * (1.0 - output * output)
    grad_hidden = propagate(grad_mixed)
    theta_grad = jnp.dot(feats.T, grad_hidden, precision=lax.Precision.HIGHEST)
    return (output.T, theta_grad)
```

```python
import functools

import jax
import jax.numpy as jnp
from jax import lax
from jax.experimental import pallas as pl
from jax.experimental.pallas import tpu as pltpu
from jax.sharding import PartitionSpec as P

BLK = 64
MB_DEV = 16
RB_DEV = 16
CAP = 2
MC = MB_DEV * BLK
RC = RB_DEV * BLK
SL = CAP * BLK
MESH = pl.DeviceIdType.MESH
F32 = jnp.float32
BF16 = jnp.bfloat16
NN = (((1,), (0,)), ((), ()))
NT = (((1,), (1,)), ((), ()))


def mm(a, b, dims):
    return lax.dot_general(a, b, dims, preferred_element_type=F32)


def split(v):
    hi = v.astype(BF16)
    lo = (v - hi.astype(F32)).astype(BF16)
    return hi, lo


def stack(v):
    return jnp.concatenate(split(v), axis=0)


def fold(p):
    half = p.shape[0] // 2
    return p[:half] + p[half:]


def local_kernel(mol_ref, rxn_ref, tiles_ref, h_ref):
    h_ref[...] = jnp.zeros_like(h_ref)
    half = lax.broadcasted_iota(jnp.int32, (BLK, 2 * BLK), 1) // BLK

    def place(k, carry):
        mol = mol_ref[k]
        rxn = rxn_ref[k]
        rows = pl.ds(pl.multiple_of(mol * BLK, BLK), BLK)
        cols = pl.ds(pl.multiple_of((rxn // 2) * 2 * BLK, 2 * BLK), 2 * BLK)
        tile = jnp.where(half == rxn % 2, tiles_ref[k].astype(F32), 0.0)
        h_ref[rows, cols] = (h_ref[rows, cols].astype(F32) + tile).astype(BF16)
        return carry

    lax.fori_loop(0, tiles_ref.shape[0], place, 0)


def main_kernel(
    n, nf, gs,
    x_ref, tht_ref, cot_ref, h_ref, t_ref, ids_ref,
    out_ref, grad_ref,
    gx, xh, xl, smat, emat, metas, metar, sbuf, rbuf, gsend, grecv, gsum, gfull,
    gx_s, gx_r, meta_s, meta_r, a2a_s, a2a_r, gr_s, gr_r, ga_s, ga_r,
):
    me = lax.axis_index("rows")
    fid = lax.axis_index("feat")
    groups = n // gs
    gw = gs * SL
    w = x_ref.shape[0]

    def each(count, body):
        if count == 1:
            body(0)
        else:
            def step(i, c):
                body(i)
                return c
            lax.fori_loop(0, count, step, 0)

    def peers(body):
        def step(k, c):
            body(lax.rem(me + k, n))
            return c
        lax.fori_loop(1, n, step, 0)

    barrier = pltpu.get_barrier_semaphore()
    peers(lambda d: pl.semaphore_signal(barrier, inc=1, device_id={"rows": d}, device_id_type=MESH))
    for k in range(1, nf):
        pl.semaphore_signal(
            barrier, inc=1, device_id={"feat": lax.rem(fid + k, nf)}, device_id_type=MESH
        )

    counts = jnp.sum(t_ref[...], axis=0, keepdims=True).astype(jnp.int32)
    first = lax.broadcasted_iota(jnp.int32, (8, SL), 0) == 0
    for d in range(n):
        cols = slice(d * SL, (d + 1) * SL)
        metas[d] = jnp.where(first, counts[:, cols], ids_ref[1:2, cols])
    pl.semaphore_wait(barrier, n - 1 + nf - 1)

    def feat_copy(src, dst, i, to):
        return pltpu.make_async_remote_copy(
            src_ref=src, dst_ref=dst, send_sem=gx_s.at[i], recv_sem=gx_r.at[i],
            device_id={"feat": to}, device_id_type=MESH,
        )

    relay = nf == 4
    hw = w // 2
    if relay:
        near = fid + 1 - 2 * lax.rem(fid, 2)
        far = lax.rem(fid + 2, 4)
        cross = lax.rem(near + 2, 4)
        rows2 = [pl.ds(0, hw), pl.ds(hw, hw)]
        c_far = [feat_copy(x_ref.at[r], gx.at[fid, r], 1 + i, far) for i, r in enumerate(rows2)]
        c_near = feat_copy(x_ref, gx.at[fid], 0, near)
        for c in c_far:
            c.start()
        c_near.start()
    else:
        direct = []
        for k in range(1, nf):
            direct.append(feat_copy(x_ref, gx.at[fid], k - 1, lax.rem(fid + k, nf)))
        for c in direct:
            c.start()

    def meta_copy(d, slot):
        return pltpu.make_async_remote_copy(
            src_ref=metas.at[d], dst_ref=metar.at[slot], send_sem=meta_s.at[d],
            recv_sem=meta_r.at[slot], device_id={"rows": d}, device_id_type=MESH,
        )

    peers(lambda d: meta_copy(d, me).start())
    metar[me] = metas[me]

    def fill_s(g):
        cols = pl.ds(pl.multiple_of(g * gw, SL), gw)
        tile = t_ref[:, cols]
        place = ids_ref[0:1, cols]
        for m in range(MB_DEV):
            smat[g, m * BLK:(m + 1) * BLK, :] = jnp.where(place == m, tile, 0.0).astype(BF16)

    each(groups, fill_s)

    ones = jnp.ones((16, MC), BF16)
    vdeg = 1.0 + mm(ones, h_ref[...], NT)
    if groups == 1:
        vdeg = vdeg + mm(jnp.ones((16, gw), BF16), smat[0], NT)
    else:
        vdeg = lax.fori_loop(
            0, groups, lambda g, v: v + mm(jnp.ones((16, gw), BF16), smat[g], NT), vdeg
        )
    vscale = (1.0 / jnp.sqrt(vdeg))[0:1]
    edeg = 1.0 + mm(ones, h_ref[...], NN)

    def split_in(f, v):
        hi, lo = split(v)
        at = pl.ds(pl.multiple_of(f * w, 16), w)
        xh[at, :] = hi
        xl[at, :] = lo

    split_in(fid, x_ref[...])

    if relay:
        c_fwd = []
        for i, r in enumerate(rows2):
            c_far[i].wait_recv()
            c = feat_copy(gx.at[far, r], gx.at[far, r], 3 + i, near)
            c.start()
            c_fwd.append(c)

    peers(lambda d: meta_copy(d, d).wait())
    state = [edeg]

    def fill_e(g, deg):
        for dd in range(gs):
            tgt = metar[g * gs + dd][1:2]
            rows = lax.broadcasted_iota(jnp.int32, (RC, SL), 0)
            emat[g, :, dd * SL:(dd + 1) * SL] = jnp.where(rows == tgt, 1.0, 0.0).astype(BF16)
        cnt = jnp.concatenate([metar[g * gs + dd] for dd in range(gs)], axis=1)
        cnt = jnp.broadcast_to(cnt[0:1], (16, gw)).astype(F32).astype(BF16)
        return deg + mm(cnt, emat[g], NT)

    if groups == 1:
        edeg = fill_e(0, edeg)
    else:
        edeg = lax.fori_loop(0, groups, fill_e, edeg)
    edeg = edeg[0:1]

    if relay:
        split_in(far, gx[far])
        c_near.wait_recv()
        split_in(near, gx[near])
        for c in c_fwd:
            c.wait_recv()
        split_in(cross, gx[cross])
        for c in [c_near] + c_far + c_fwd:
            c.wait_send()
    else:
        for k, c in enumerate(direct):
            c.wait()
            src = lax.rem(fid + nf - k - 1, nf)
            split_in(src, gx[src])

    th, tl = split(tht_ref[...])
    hidden = fold(mm(jnp.concatenate([th, tl], axis=0), xh[...], NN)) + mm(th, xl[...], NN)

    def a2a(phase, d, slot):
        return pltpu.make_async_remote_copy(
            src_ref=sbuf.at[phase, d], dst_ref=rbuf.at[phase, slot],
            send_sem=a2a_s.at[phase, d], recv_sem=a2a_r.at[phase, slot],
            device_id={"rows": d}, device_id_type=MESH,
        )

    def exchange(phase, lhs, mat):
        def part(g):
            p = fold(mm(lhs, mat[g], NN))
            for dd in range(gs):
                sbuf[phase, g * gs + dd] = p[:, dd * SL:(dd + 1) * SL]

        each(groups, part)
        peers(lambda d: a2a(phase, d, me).start())
        rbuf[phase, me] = sbuf[phase, me]

    def collect(phase, acc, mat):
        peers(lambda d: a2a(phase, d, d).wait())

        def add(g, a):
            got = jnp.concatenate([rbuf[phase, g * gs + dd] for dd in range(gs)], axis=1)
            return a + fold(mm(stack(got), mat[g], NT))

        if groups == 1:
            return add(0, acc)
        return lax.fori_loop(0, groups, add, acc)

    def propagate(values, phase):
        lhs = stack(values * vscale)
        exchange(phase, lhs, smat)
        acc = fold(mm(lhs, h_ref[...], NN))
        edge = collect(phase, acc, emat) / edeg
        lhs = stack(edge)
        exchange(phase + 1, lhs, emat)
        acc = fold(mm(lhs, h_ref[...], NT))
        return collect(phase + 1, acc, smat) * vscale

    output = jnp.tanh(propagate(hidden, 0))
    out_ref[...] = output
    gh, gl = split(propagate(cot_ref[...] * (1.0 - output * output), 2))
    partial = fold(mm(jnp.concatenate([gh, gl], axis=0), xh[...], NT)) + mm(gh, xl[...], NT)

    k = w // n
    for d in range(n):
        gsend[d] = partial[d * k:(d + 1) * k]

    def gr(d, slot):
        return pltpu.make_async_remote_copy(
            src_ref=gsend.at[d], dst_ref=grecv.at[slot], send_sem=gr_s.at[d],
            recv_sem=gr_r.at[slot], device_id={"rows": d}, device_id_type=MESH,
        )

    peers(lambda d: gr(d, me).start())
    grecv[me] = gsend[me]
    peers(lambda d: gr(d, d).wait())
    gsum[...] = jnp.sum(grecv[...], axis=0)

    def ga(d, slot):
        return pltpu.make_async_remote_copy(
            src_ref=gsum, dst_ref=gfull.at[slot], send_sem=ga_s.at[d],
            recv_sem=ga_r.at[slot], device_id={"rows": d}, device_id_type=MESH,
        )

    peers(lambda d: ga(d, me).start())
    gfull[me] = gsum[...]
    peers(lambda d: ga(d, d).wait())
    grad_ref[...] = gfull[...]


def on_device(
    node_feats, theta, cotangent, remote_mol, remote_rxn, remote_count, remote_tiles,
    local_mol, local_rxn, local_tiles,
):
    n = lax.axis_size("rows")
    nf = lax.axis_size("feat")
    gs = min(n, 8)
    groups = n // gs
    gw = gs * SL
    slots = n * CAP
    w, mols = node_feats.shape
    f = w * nf
    vmem = pl.BlockSpec(memory_space=pltpu.VMEM)
    smem = pl.BlockSpec(memory_space=pltpu.SMEM)

    ltiles = local_tiles.reshape(-1, BLK, BLK).astype(BF16)
    ltiles = jnp.concatenate([ltiles, ltiles], axis=2)
    dense = pl.pallas_call(
        local_kernel,
        out_shape=jax.ShapeDtypeStruct((MC, RC), BF16),
        in_specs=[smem, smem, vmem],
        out_specs=vmem,
        compiler_params=pltpu.CompilerParams(vmem_limit_bytes=16 * 2**20),
        name="local_incidence",
    )(local_mol, local_rxn, ltiles)

    live = (jnp.arange(CAP, dtype=jnp.int32)[None, :] < remote_count[:, None]).reshape(slots)
    rtiles = remote_tiles.reshape(slots, BLK, BLK).astype(F32)
    rtiles = jnp.where(live[:, None, None], rtiles, 0.0)
    rtiles = rtiles.transpose(1, 0, 2).reshape(BLK, slots * BLK)
    place = jnp.broadcast_to(remote_mol.reshape(slots, 1), (slots, BLK)).reshape(1, -1)
    target = (remote_rxn.reshape(slots, 1) * BLK + jnp.arange(BLK, dtype=jnp.int32)).reshape(1, -1)
    ids = jnp.concatenate([place, target], axis=0)

    dma = pltpu.SemaphoreType.DMA
    out, grad = pl.pallas_call(
        functools.partial(main_kernel, n, nf, gs),
        out_shape=(
            jax.ShapeDtypeStruct((w, mols), F32),
            jax.ShapeDtypeStruct((n, w // n, f), F32),
        ),
        in_specs=[vmem] * 6,
        out_specs=(vmem, vmem),
        scratch_shapes=[
            pltpu.VMEM((nf, w, mols), F32),
            pltpu.VMEM((f, mols), BF16),
            pltpu.VMEM((f, mols), BF16),
            pltpu.VMEM((groups, MC, gw), BF16),
            pltpu.VMEM((groups, RC, gw), BF16),
            pltpu.VMEM((n, 8, SL), jnp.int32),
            pltpu.VMEM((n, 8, SL), jnp.int32),
            pltpu.VMEM((4, n, w, SL), F32),
            pltpu.VMEM((4, n, w, SL), F32),
            pltpu.VMEM((n, w // n, f), F32),
            pltpu.VMEM((n, w // n, f), F32),
            pltpu.VMEM((w // n, f), F32),
            pltpu.VMEM((n, w // n, f), F32),
            dma((max(nf, 5),)), dma((max(nf, 5),)),
            dma((n,)), dma((n,)),
            dma((4, n)), dma((4, n)),
            dma((n,)), dma((n,)),
            dma((n,)), dma((n,)),
        ],
        compiler_params=pltpu.CompilerParams(
            collective_id=0, has_side_effects=True,
            vmem_limit_bytes=(28 + n // 2) * 2**20,
        ),
        name="train_step",
    )(node_feats, theta.T, cotangent, dense, rtiles, ids)
    return out, grad.reshape(w, f).T


def solution(mesh):
    return jax.shard_map(
        on_device,
        mesh=mesh,
        in_specs=(
            P("feat", "rows"),
            P(None, "feat"),
            P("feat", "rows"),
            P("rows", None),
            P("rows", None),
            P("rows"),
            P("rows", None, None),
            P("rows"),
            P("rows"),
            P("rows", None),
        ),
        out_specs=(P("feat", "rows"), P(None, "feat")),
        check_vma=False,
    )
```

```python
import functools

import jax
import jax.numpy as jnp
from jax import lax
from jax.experimental import pallas as pl
from jax.experimental.pallas import tpu as pltpu
from jax.sharding import PartitionSpec as P

BLK = 64
MB_DEV = 16
RB_DEV = 16
CAP = 2
PARTS = 2
MC = MB_DEV * BLK
RC = RB_DEV * BLK
SL = CAP * BLK
MESH = pl.DeviceIdType.MESH
F32 = jnp.float32
BF16 = jnp.bfloat16
NN = (((1,), (0,)), ((), ()))
NT = (((1,), (1,)), ((), ()))


def mm(a, b, dims):
    return lax.dot_general(a, b, dims, preferred_element_type=F32)


def split(v):
    hi = v.astype(BF16)
    lo = (v - hi.astype(F32)).astype(BF16)
    return hi, lo


def stack(v):
    return jnp.concatenate(split(v), axis=0)


def fold(p):
    half = p.shape[0] // 2
    return p[:half] + p[half:]


def local_kernel(mol_ref, rxn_ref, tiles_ref, h_ref):
    h_ref[...] = jnp.zeros_like(h_ref)
    half = lax.broadcasted_iota(jnp.int32, (BLK, 2 * BLK), 1) // BLK

    def place(k, carry):
        mol = mol_ref[k]
        rxn = rxn_ref[k]
        rows = pl.ds(pl.multiple_of(mol * BLK, BLK), BLK)
        cols = pl.ds(pl.multiple_of((rxn // 2) * 2 * BLK, 2 * BLK), 2 * BLK)
        tile = jnp.where(half == rxn % 2, tiles_ref[k].astype(F32), 0.0)
        h_ref[rows, cols] = (h_ref[rows, cols].astype(F32) + tile).astype(BF16)
        return carry

    lax.fori_loop(0, tiles_ref.shape[0], place, 0)


def main_kernel(
    n, nf, gs,
    x_ref, tht_ref, cot_ref, h_ref, t_ref, ids_ref,
    out_ref, grad_ref,
    gx, xh, xl, smat, emat, metas, metar, sbuf, rbuf, gsend, grecv, gsum, gfull,
    gx_s, gx_r, meta_s, meta_r, a2a_s, a2a_r, gr_s, gr_r, ga_s, ga_r,
):
    me = lax.axis_index("rows")
    fid = lax.axis_index("feat")
    groups = n // gs
    gw = gs * SL
    w = x_ref.shape[0]

    def each(count, body):
        if count == 1:
            body(0)
        else:
            def step(i, c):
                body(i)
                return c
            lax.fori_loop(0, count, step, 0)

    def peers(body):
        def step(k, c):
            body(lax.rem(me + k, n))
            return c
        lax.fori_loop(1, n, step, 0)

    barrier = pltpu.get_barrier_semaphore()
    peers(lambda d: pl.semaphore_signal(barrier, inc=1, device_id={"rows": d}, device_id_type=MESH))
    for k in range(1, nf):
        pl.semaphore_signal(
            barrier, inc=1, device_id={"feat": lax.rem(fid + k, nf)}, device_id_type=MESH
        )

    counts = jnp.sum(t_ref[...], axis=0, keepdims=True).astype(jnp.int32)
    first = lax.broadcasted_iota(jnp.int32, (8, SL), 0) == 0
    for d in range(n):
        cols = slice(d * SL, (d + 1) * SL)
        metas[d] = jnp.where(first, counts[:, cols], ids_ref[1:2, cols])

    def meta_copy(d, slot):
        return pltpu.make_async_remote_copy(
            src_ref=metas.at[d], dst_ref=metar.at[slot], send_sem=meta_s.at[d],
            recv_sem=meta_r.at[slot], device_id={"rows": d}, device_id_type=MESH,
        )

    def fill_s(g):
        cols = pl.ds(pl.multiple_of(g * gw, SL), gw)
        tile = t_ref[:, cols]
        place = ids_ref[0:1, cols]
        for m in range(MB_DEV):
            smat[g, m * BLK:(m + 1) * BLK, :] = jnp.where(place == m, tile, 0.0).astype(BF16)

    each(groups, fill_s)

    ones = jnp.ones((16, MC), BF16)
    vdeg = 1.0 + mm(ones, h_ref[...], NT)
    if groups == 1:
        vdeg = vdeg + mm(jnp.ones((16, gw), BF16), smat[0], NT)
    else:
        vdeg = lax.fori_loop(
            0, groups, lambda g, v: v + mm(jnp.ones((16, gw), BF16), smat[g], NT), vdeg
        )
    vscale = (1.0 / jnp.sqrt(vdeg))[0:1]

    hw = w // PARTS
    parts = [slice(i * hw, (i + 1) * hw) for i in range(PARTS)]

    def a2a(phase, i, d, slot):
        return pltpu.make_async_remote_copy(
            src_ref=sbuf.at[phase, i, d], dst_ref=rbuf.at[phase, i, slot],
            send_sem=a2a_s.at[phase, i, d], recv_sem=a2a_r.at[phase, i, slot],
            device_id={"rows": d}, device_id_type=MESH,
        )

    def produce(phase, i, lhs, mat):
        def part(g):
            p = fold(mm(lhs, mat[g], NN))
            for dd in range(gs):
                sbuf[phase, i, g * gs + dd] = p[:, dd * SL:(dd + 1) * SL]

        each(groups, part)

    def send(phase, i):
        peers(lambda d: a2a(phase, i, d, me).start())
        rbuf[phase, i, me] = sbuf[phase, i, me]

    def collect(phase, i, acc, mat):
        peers(lambda d: a2a(phase, i, d, d).wait())

        def add(g, a):
            got = jnp.concatenate([rbuf[phase, i, g * gs + dd] for dd in range(gs)], axis=1)
            return a + fold(mm(stack(got), mat[g], NT))

        if groups == 1:
            return add(0, acc)
        return lax.fori_loop(0, groups, add, acc)

    lhs = [stack(x_ref[p, :] * vscale) for p in parts]
    produce(0, 0, lhs[0], smat)
    pl.semaphore_wait(barrier, n - 1 + nf - 1)
    peers(lambda d: meta_copy(d, me).start())
    metar[me] = metas[me]
    send(0, 0)
    for i in range(1, PARTS):
        produce(0, i, lhs[i], smat)
        send(0, i)

    edeg = 1.0 + mm(ones, h_ref[...], NN)
    acc = [fold(mm(v, h_ref[...], NN)) for v in lhs]
    peers(lambda d: meta_copy(d, d).wait())

    def fill_e(g, deg):
        for dd in range(gs):
            tgt = metar[g * gs + dd][1:2]
            rows = lax.broadcasted_iota(jnp.int32, (RC, SL), 0)
            emat[g, :, dd * SL:(dd + 1) * SL] = jnp.where(rows == tgt, 1.0, 0.0).astype(BF16)
        cnt = jnp.concatenate([metar[g * gs + dd] for dd in range(gs)], axis=1)
        cnt = jnp.broadcast_to(cnt[0:1], (16, gw)).astype(F32).astype(BF16)
        return deg + mm(cnt, emat[g], NT)

    if groups == 1:
        edeg = fill_e(0, edeg)
    else:
        edeg = lax.fori_loop(0, groups, fill_e, edeg)
    edeg = edeg[0:1]

    lhs = []
    for i in range(PARTS):
        lhs.append(stack(collect(0, i, acc[i], emat) / edeg))
        produce(1, i, lhs[i], emat)
        send(1, i)
    acc = [fold(mm(v, h_ref[...], NT)) for v in lhs]

    def feat_copy(slot, p, i, to):
        ref = gx.at[slot, pl.ds(p * hw, hw)]
        return pltpu.make_async_remote_copy(
            src_ref=ref, dst_ref=ref, send_sem=gx_s.at[i, p], recv_sem=gx_r.at[i, p],
            device_id={"feat": to}, device_id_type=MESH,
        )

    def split_in(f, p):
        hi, lo = split(gx[f, p * hw:(p + 1) * hw, :])
        at = pl.ds(pl.multiple_of(f * w + p * hw, 16), hw)
        xh[at, :] = hi
        xl[at, :] = lo

    relay = nf == 4
    near = fid + 1 - 2 * lax.rem(fid, 2)
    far = lax.rem(fid + 2, nf)
    cross = lax.rem(near + 2, nf)
    sent = []
    for i in range(PARTS):
        gx[fid, parts[i], :] = collect(1, i, acc[i], smat) * vscale
        if relay:
            c = [feat_copy(fid, i, 0, far), feat_copy(fid, i, 1, near)]
        else:
            c = [feat_copy(fid, i, k - 1, lax.rem(fid + k, nf)) for k in range(1, nf)]
        for one in c:
            one.start()
        sent.append(c)
    for i in range(PARTS):
        split_in(fid, i)
    if relay:
        passed = []
        for i in range(PARTS):
            sent[i][0].wait_recv()
            c = feat_copy(far, i, 2, near)
            c.start()
            passed.append(c)
            split_in(far, i)
            sent[i][1].wait_recv()
            split_in(near, i)
        for i in range(PARTS):
            passed[i].wait_recv()
            split_in(cross, i)
        for c in passed + sum(sent, []):
            c.wait_send()
    else:
        for i in range(PARTS):
            for k, c in enumerate(sent[i]):
                c.wait()
                split_in(lax.rem(fid + nf - k - 1, nf), i)

    th, tl = split(tht_ref[...])
    mixed = fold(mm(jnp.concatenate([th, tl], axis=0), xh[...], NN)) + mm(th, xl[...], NN)
    output = jnp.tanh(mixed)
    out_ref[...] = output
    gh, gl = split(cot_ref[...] * (1.0 - output * output))
    partial = fold(mm(jnp.concatenate([gh, gl], axis=0), xh[...], NT)) + mm(gh, xl[...], NT)

    k = w // n
    for d in range(n):
        gsend[d] = partial[d * k:(d + 1) * k]

    def gr(d, slot):
        return pltpu.make_async_remote_copy(
            src_ref=gsend.at[d], dst_ref=grecv.at[slot], send_sem=gr_s.at[d],
            recv_sem=gr_r.at[slot], device_id={"rows": d}, device_id_type=MESH,
        )

    peers(lambda d: gr(d, me).start())
    grecv[me] = gsend[me]
    peers(lambda d: gr(d, d).wait())
    gsum[...] = jnp.sum(grecv[...], axis=0)

    def ga(d, slot):
        return pltpu.make_async_remote_copy(
            src_ref=gsum, dst_ref=gfull.at[slot], send_sem=ga_s.at[d],
            recv_sem=ga_r.at[slot], device_id={"rows": d}, device_id_type=MESH,
        )

    peers(lambda d: ga(d, me).start())
    gfull[me] = gsum[...]
    peers(lambda d: ga(d, d).wait())
    grad_ref[...] = gfull[...]


def on_device(
    node_feats, theta, cotangent, remote_mol, remote_rxn, remote_count, remote_tiles,
    local_mol, local_rxn, local_tiles,
):
    n = lax.axis_size("rows")
    nf = lax.axis_size("feat")
    gs = min(n, 8)
    groups = n // gs
    gw = gs * SL
    slots = n * CAP
    w, mols = node_feats.shape
    f = w * nf
    vmem = pl.BlockSpec(memory_space=pltpu.VMEM)
    smem = pl.BlockSpec(memory_space=pltpu.SMEM)

    ltiles = local_tiles.reshape(-1, BLK, BLK).astype(BF16)
    ltiles = jnp.concatenate([ltiles, ltiles], axis=2)
    dense = pl.pallas_call(
        local_kernel,
        out_shape=jax.ShapeDtypeStruct((MC, RC), BF16),
        in_specs=[smem, smem, vmem],
        out_specs=vmem,
        compiler_params=pltpu.CompilerParams(vmem_limit_bytes=16 * 2**20),
        name="local_incidence",
    )(local_mol, local_rxn, ltiles)

    live = (jnp.arange(CAP, dtype=jnp.int32)[None, :] < remote_count[:, None]).reshape(slots)
    rtiles = remote_tiles.reshape(slots, BLK, BLK).astype(F32)
    rtiles = jnp.where(live[:, None, None], rtiles, 0.0)
    rtiles = rtiles.transpose(1, 0, 2).reshape(BLK, slots * BLK)
    place = jnp.broadcast_to(remote_mol.reshape(slots, 1), (slots, BLK)).reshape(1, -1)
    target = (remote_rxn.reshape(slots, 1) * BLK + jnp.arange(BLK, dtype=jnp.int32)).reshape(1, -1)
    ids = jnp.concatenate([place, target], axis=0)

    dma = pltpu.SemaphoreType.DMA
    out, grad = pl.pallas_call(
        functools.partial(main_kernel, n, nf, gs),
        out_shape=(
            jax.ShapeDtypeStruct((w, mols), F32),
            jax.ShapeDtypeStruct((n, w // n, f), F32),
        ),
        in_specs=[vmem] * 6,
        out_specs=(vmem, vmem),
        scratch_shapes=[
            pltpu.VMEM((nf, w, mols), F32),
            pltpu.VMEM((f, mols), BF16),
            pltpu.VMEM((f, mols), BF16),
            pltpu.VMEM((groups, MC, gw), BF16),
            pltpu.VMEM((groups, RC, gw), BF16),
            pltpu.VMEM((n, 8, SL), jnp.int32),
            pltpu.VMEM((n, 8, SL), jnp.int32),
            pltpu.VMEM((2, PARTS, n, w // PARTS, SL), F32),
            pltpu.VMEM((2, PARTS, n, w // PARTS, SL), F32),
            pltpu.VMEM((n, w // n, f), F32),
            pltpu.VMEM((n, w // n, f), F32),
            pltpu.VMEM((w // n, f), F32),
            pltpu.VMEM((n, w // n, f), F32),
            dma((max(nf - 1, 3), PARTS)), dma((max(nf - 1, 3), PARTS)),
            dma((n,)), dma((n,)),
            dma((2, PARTS, n)), dma((2, PARTS, n)),
            dma((n,)), dma((n,)),
            dma((n,)), dma((n,)),
        ],
        compiler_params=pltpu.CompilerParams(
            collective_id=0, has_side_effects=True,
            vmem_limit_bytes=(28 + n // 2) * 2**20,
        ),
        name="train_step",
    )(node_feats, theta.T, cotangent, dense, rtiles, ids)
    return out, grad.reshape(w, f).T


def solution(mesh):
    return jax.shard_map(
        on_device,
        mesh=mesh,
        in_specs=(
            P("feat", "rows"),
            P(None, "feat"),
            P("feat", "rows"),
            P("rows", None),
            P("rows", None),
            P("rows"),
            P("rows", None, None),
            P("rows"),
            P("rows"),
            P("rows", None),
        ),
        out_specs=(P("feat", "rows"), P(None, "feat")),
        check_vma=False,
    )
```

```python
import functools

import jax
import jax.numpy as jnp
from jax import lax
from jax.experimental import pallas as pl
from jax.experimental.pallas import tpu as pltpu
from jax.sharding import PartitionSpec as P

BLK = 64
MB_DEV = 16
RB_DEV = 16
CAP = 2
PARTS = 2
MC = MB_DEV * BLK
RC = RB_DEV * BLK
SL = CAP * BLK
MESH = pl.DeviceIdType.MESH
F32 = jnp.float32
BF16 = jnp.bfloat16
NN = (((1,), (0,)), ((), ()))
NT = (((1,), (1,)), ((), ()))


def mm(a, b, dims):
    return lax.dot_general(a, b, dims, preferred_element_type=F32)


def split(v):
    hi = v.astype(BF16)
    lo = (v - hi.astype(F32)).astype(BF16)
    return hi, lo


def stack(v):
    return jnp.concatenate(split(v), axis=0)


def fold(p):
    half = p.shape[0] // 2
    return p[:half] + p[half:]


def local_kernel(mol_ref, rxn_ref, tiles_ref, h_ref):
    h_ref[...] = jnp.zeros_like(h_ref)
    half = lax.broadcasted_iota(jnp.int32, (BLK, 2 * BLK), 1) // BLK

    def place(k, carry):
        mol = mol_ref[k]
        rxn = rxn_ref[k]
        rows = pl.ds(pl.multiple_of(mol * BLK, BLK), BLK)
        cols = pl.ds(pl.multiple_of((rxn // 2) * 2 * BLK, 2 * BLK), 2 * BLK)
        tile = jnp.where(half == rxn % 2, tiles_ref[k].astype(F32), 0.0)
        h_ref[rows, cols] = (h_ref[rows, cols].astype(F32) + tile).astype(BF16)
        return carry

    lax.fori_loop(0, tiles_ref.shape[0], place, 0, unroll=4)


def main_kernel(
    n, nf, gs,
    x_ref, tht_ref, cot_ref, h_ref, t_ref, mol_ref, rxn_ref, cnt_ref,
    out_ref, grad_ref,
    gx, xh, xl, smat, emat, metas, metar, sbuf, rbuf, gsend, grecv, gsum, gfull,
    gx_s, gx_r, meta_s, meta_r, a2a_s, a2a_r, gr_s, gr_r, ga_s, ga_r,
):
    me = lax.axis_index("rows")
    fid = lax.axis_index("feat")
    groups = n // gs
    gw = gs * SL
    w = x_ref.shape[0]

    def each(count, body):
        if count == 1:
            body(0)
        else:
            def step(i, c):
                body(i)
                return c
            lax.fori_loop(0, count, step, 0)

    def peers(body):
        def step(k, c):
            body(lax.rem(me + k, n))
            return c
        lax.fori_loop(1, n, step, 0)

    barrier = pltpu.get_barrier_semaphore()
    peers(lambda d: pl.semaphore_signal(barrier, inc=1, device_id={"rows": d}, device_id_type=MESH))
    for k in range(1, nf):
        pl.semaphore_signal(
            barrier, inc=1, device_id={"feat": lax.rem(fid + k, nf)}, device_id_type=MESH
        )

    first = lax.broadcasted_iota(jnp.int32, (8, SL), 0) == 0
    lane = lax.broadcasted_iota(jnp.int32, (1, SL), 1)
    slot = lane // BLK
    for d in range(n):
        live = slot < cnt_ref[d]
        place = jnp.where(live, jnp.where(slot == 0, mol_ref[0, d], mol_ref[1, d]), -1)
        target = jnp.where(slot == 0, rxn_ref[0, d], rxn_ref[1, d]) * BLK + lane % BLK
        tile = jnp.where(live, t_ref[:, d * SL:(d + 1) * SL], 0.0)
        counts = jnp.sum(tile, axis=0, keepdims=True).astype(jnp.int32)
        metas[d] = jnp.where(first, counts, target)
        at = slice((d % gs) * SL, (d % gs + 1) * SL)
        for m in range(MB_DEV):
            here = jnp.where(place == m, tile, 0.0)
            smat[d // gs, m * BLK:(m + 1) * BLK, at] = here.astype(BF16)

    def meta_copy(d, slot):
        return pltpu.make_async_remote_copy(
            src_ref=metas.at[d], dst_ref=metar.at[slot], send_sem=meta_s.at[d],
            recv_sem=meta_r.at[slot], device_id={"rows": d}, device_id_type=MESH,
        )

    ones = jnp.ones((16, MC), BF16)
    vdeg = 1.0 + mm(ones, h_ref[...], NT)
    if groups == 1:
        vdeg = vdeg + mm(jnp.ones((16, gw), BF16), smat[0], NT)
    else:
        vdeg = lax.fori_loop(
            0, groups, lambda g, v: v + mm(jnp.ones((16, gw), BF16), smat[g], NT), vdeg
        )
    vscale = (1.0 / jnp.sqrt(vdeg))[0:1]

    hw = w // PARTS
    parts = [slice(i * hw, (i + 1) * hw) for i in range(PARTS)]

    def a2a(phase, i, d, slot):
        return pltpu.make_async_remote_copy(
            src_ref=sbuf.at[phase, i, d], dst_ref=rbuf.at[phase, i, slot],
            send_sem=a2a_s.at[phase, i, d], recv_sem=a2a_r.at[phase, i, slot],
            device_id={"rows": d}, device_id_type=MESH,
        )

    def produce(phase, i, lhs, mat):
        def part(g):
            p = fold(mm(lhs, mat[g], NN))
            for dd in range(gs):
                sbuf[phase, i, g * gs + dd] = p[:, dd * SL:(dd + 1) * SL]

        each(groups, part)

    def send(phase, i):
        peers(lambda d: a2a(phase, i, d, me).start())
        rbuf[phase, i, me] = sbuf[phase, i, me]

    def collect(phase, i, acc, mat):
        peers(lambda d: a2a(phase, i, d, d).wait())

        def add(g, a):
            got = jnp.concatenate([rbuf[phase, i, g * gs + dd] for dd in range(gs)], axis=1)
            return a + fold(mm(stack(got), mat[g], NT))

        if groups == 1:
            return add(0, acc)
        return lax.fori_loop(0, groups, add, acc)

    lhs = [stack(x_ref[p, :] * vscale) for p in parts]
    for i in range(PARTS):
        produce(0, i, lhs[i], smat)
    edeg = 1.0 + mm(ones, h_ref[...], NN)
    acc = [fold(mm(v, h_ref[...], NN)) for v in lhs]
    pl.semaphore_wait(barrier, n - 1 + nf - 1)
    peers(lambda d: meta_copy(d, me).start())
    metar[me] = metas[me]
    for i in range(PARTS):
        send(0, i)

    peers(lambda d: meta_copy(d, d).wait())

    def fill_e(g, deg):
        for dd in range(gs):
            tgt = metar[g * gs + dd][1:2]
            rows = lax.broadcasted_iota(jnp.int32, (RC, SL), 0)
            emat[g, :, dd * SL:(dd + 1) * SL] = jnp.where(rows == tgt, 1.0, 0.0).astype(BF16)
        cnt = jnp.concatenate([metar[g * gs + dd] for dd in range(gs)], axis=1)
        cnt = jnp.broadcast_to(cnt[0:1], (16, gw)).astype(F32).astype(BF16)
        return deg + mm(cnt, emat[g], NT)

    if groups == 1:
        edeg = fill_e(0, edeg)
    else:
        edeg = lax.fori_loop(0, groups, fill_e, edeg)
    edeg = edeg[0:1]

    lhs = []
    for i in range(PARTS):
        lhs.append(stack(collect(0, i, acc[i], emat) / edeg))
        produce(1, i, lhs[i], emat)
        send(1, i)
    acc = [fold(mm(v, h_ref[...], NT)) for v in lhs]

    def feat_copy(slot, p, i, to):
        ref = gx.at[slot, pl.ds(p * hw, hw)]
        return pltpu.make_async_remote_copy(
            src_ref=ref, dst_ref=ref, send_sem=gx_s.at[i, p], recv_sem=gx_r.at[i, p],
            device_id={"feat": to}, device_id_type=MESH,
        )

    def split_in(f, p):
        hi, lo = split(gx[f, p * hw:(p + 1) * hw, :])
        at = pl.ds(pl.multiple_of(f * w + p * hw, 16), hw)
        xh[at, :] = hi
        xl[at, :] = lo

    relay = nf == 4
    near = fid + 1 - 2 * lax.rem(fid, 2)
    far = lax.rem(fid + 2, nf)
    cross = lax.rem(near + 2, nf)
    sent = []
    for i in range(PARTS):
        gx[fid, parts[i], :] = collect(1, i, acc[i], smat) * vscale
        if relay:
            c = [feat_copy(fid, i, 0, far), feat_copy(fid, i, 1, near)]
        else:
            c = [feat_copy(fid, i, k - 1, lax.rem(fid + k, nf)) for k in range(1, nf)]
        for one in c:
            one.start()
        sent.append(c)
    for i in range(PARTS):
        split_in(fid, i)
    if relay:
        passed = []
        for i in range(PARTS):
            sent[i][0].wait_recv()
            c = feat_copy(far, i, 2, near)
            c.start()
            passed.append(c)
            split_in(far, i)
            sent[i][1].wait_recv()
            split_in(near, i)
        for i in range(PARTS):
            passed[i].wait_recv()
            split_in(cross, i)
        for c in passed + sum(sent, []):
            c.wait_send()
    else:
        for i in range(PARTS):
            for k, c in enumerate(sent[i]):
                c.wait()
                split_in(lax.rem(fid + nf - k - 1, nf), i)

    th, tl = split(tht_ref[...])
    mixed = fold(mm(jnp.concatenate([th, tl], axis=0), xh[...], NN)) + mm(th, xl[...], NN)
    output = jnp.tanh(mixed)
    out_ref[...] = output
    gh, gl = split(cot_ref[...] * (1.0 - output * output))
    partial = fold(mm(jnp.concatenate([gh, gl], axis=0), xh[...], NT)) + mm(gh, xl[...], NT)

    k = w // n
    for d in range(n):
        gsend[d] = partial[d * k:(d + 1) * k]

    def gr(d, slot):
        return pltpu.make_async_remote_copy(
            src_ref=gsend.at[d], dst_ref=grecv.at[slot], send_sem=gr_s.at[d],
            recv_sem=gr_r.at[slot], device_id={"rows": d}, device_id_type=MESH,
        )

    peers(lambda d: gr(d, me).start())
    grecv[me] = gsend[me]
    peers(lambda d: gr(d, d).wait())
    gsum[...] = jnp.sum(grecv[...], axis=0)

    def ga(d, slot):
        return pltpu.make_async_remote_copy(
            src_ref=gsum, dst_ref=gfull.at[slot], send_sem=ga_s.at[d],
            recv_sem=ga_r.at[slot], device_id={"rows": d}, device_id_type=MESH,
        )

    peers(lambda d: ga(d, me).start())
    gfull[me] = gsum[...]
    peers(lambda d: ga(d, d).wait())
    grad_ref[...] = gfull[...]


def on_device(
    node_feats, theta, cotangent, remote_mol, remote_rxn, remote_count, remote_tiles,
    local_mol, local_rxn, local_tiles,
):
    n = lax.axis_size("rows")
    nf = lax.axis_size("feat")
    gs = min(n, 8)
    groups = n // gs
    gw = gs * SL
    slots = n * CAP
    w, mols = node_feats.shape
    f = w * nf
    vmem = pl.BlockSpec(memory_space=pltpu.VMEM)
    smem = pl.BlockSpec(memory_space=pltpu.SMEM)

    ltiles = local_tiles.reshape(-1, BLK, BLK).astype(BF16)
    ltiles = jnp.concatenate([ltiles, ltiles], axis=2)
    dense = pl.pallas_call(
        local_kernel,
        out_shape=jax.ShapeDtypeStruct((MC, RC), BF16),
        in_specs=[smem, smem, vmem],
        out_specs=vmem,
        compiler_params=pltpu.CompilerParams(vmem_limit_bytes=16 * 2**20),
        name="local_incidence",
    )(local_mol, local_rxn, ltiles)

    rtiles = remote_tiles.reshape(slots, BLK, BLK).astype(F32)
    rtiles = rtiles.transpose(1, 0, 2).reshape(BLK, slots * BLK)

    dma = pltpu.SemaphoreType.DMA
    out, grad = pl.pallas_call(
        functools.partial(main_kernel, n, nf, gs),
        out_shape=(
            jax.ShapeDtypeStruct((w, mols), F32),
            jax.ShapeDtypeStruct((n, w // n, f), F32),
        ),
        in_specs=[vmem] * 5 + [smem] * 3,
        out_specs=(vmem, vmem),
        scratch_shapes=[
            pltpu.VMEM((nf, w, mols), F32),
            pltpu.VMEM((f, mols), BF16),
            pltpu.VMEM((f, mols), BF16),
            pltpu.VMEM((groups, MC, gw), BF16),
            pltpu.VMEM((groups, RC, gw), BF16),
            pltpu.VMEM((n, 8, SL), jnp.int32),
            pltpu.VMEM((n, 8, SL), jnp.int32),
            pltpu.VMEM((2, PARTS, n, w // PARTS, SL), F32),
            pltpu.VMEM((2, PARTS, n, w // PARTS, SL), F32),
            pltpu.VMEM((n, w // n, f), F32),
            pltpu.VMEM((n, w // n, f), F32),
            pltpu.VMEM((w // n, f), F32),
            pltpu.VMEM((n, w // n, f), F32),
            dma((max(nf - 1, 3), PARTS)), dma((max(nf - 1, 3), PARTS)),
            dma((n,)), dma((n,)),
            dma((2, PARTS, n)), dma((2, PARTS, n)),
            dma((n,)), dma((n,)),
            dma((n,)), dma((n,)),
        ],
        compiler_params=pltpu.CompilerParams(
            collective_id=0, has_side_effects=True,
            vmem_limit_bytes=(28 + n // 2) * 2**20,
        ),
        name="train_step",
    )(node_feats, theta.T, cotangent, dense, rtiles, remote_mol.T, remote_rxn.T, remote_count)
    return out, grad.reshape(w, f).T


def solution(mesh):
    return jax.shard_map(
        on_device,
        mesh=mesh,
        in_specs=(
            P("feat", "rows"),
            P(None, "feat"),
            P("feat", "rows"),
            P("rows", None),
            P("rows", None),
            P("rows"),
            P("rows", None, None),
            P("rows"),
            P("rows"),
            P("rows", None),
        ),
        out_specs=(P("feat", "rows"), P(None, "feat")),
        check_vma=False,
    )
```

```python
import functools

import jax
import jax.numpy as jnp
from jax import lax
from jax.experimental import pallas as pl
from jax.experimental.pallas import tpu as pltpu
from jax.sharding import PartitionSpec as P

BLK = 64
MB_DEV = 16
RB_DEV = 16
CAP = 2
PARTS = 2
MC = MB_DEV * BLK
RC = RB_DEV * BLK
SL = CAP * BLK
MESH = pl.DeviceIdType.MESH
F32 = jnp.float32
BF16 = jnp.bfloat16
NN = (((1,), (0,)), ((), ()))
NT = (((1,), (1,)), ((), ()))


def mm(a, b, dims):
    return lax.dot_general(a, b, dims, preferred_element_type=F32)


def split(v):
    hi = v.astype(BF16)
    lo = (v - hi.astype(F32)).astype(BF16)
    return hi, lo


def stack(v):
    return jnp.concatenate(split(v), axis=0)


def fold(p):
    half = p.shape[0] // 2
    return p[:half] + p[half:]


def local_kernel(mol_ref, rxn_ref, tiles_ref, h_ref):
    h_ref[...] = jnp.zeros_like(h_ref)
    half = lax.broadcasted_iota(jnp.int32, (BLK, 2 * BLK), 1) // BLK

    def place(k, carry):
        mol = mol_ref[k]
        rxn = rxn_ref[k]
        rows = pl.ds(pl.multiple_of(mol * BLK, BLK), BLK)
        cols = pl.ds(pl.multiple_of((rxn // 2) * 2 * BLK, 2 * BLK), 2 * BLK)
        tile = jnp.where(half == rxn % 2, tiles_ref[k].astype(F32), 0.0)
        h_ref[rows, cols] = (h_ref[rows, cols].astype(F32) + tile).astype(BF16)
        return carry

    lax.fori_loop(0, tiles_ref.shape[0], place, 0, unroll=4)


def main_kernel(
    n, nf, gs,
    x_ref, tht_ref, cot_ref, h_ref, t_ref, mol_ref, rxn_ref, cnt_ref,
    out_ref, grad_ref,
    gx, xh, xl, smat, emat, metas, metar, sbuf, rbuf, gsend, grecv, gsum, gfull,
    gx_s, gx_r, meta_s, meta_r, a2a_s, a2a_r, gr_s, gr_r, ga_s, ga_r,
):
    me = lax.axis_index("rows")
    fid = lax.axis_index("feat")
    groups = n // gs
    gw = gs * SL
    w = x_ref.shape[0]

    def each(count, body):
        if count == 1:
            body(0)
        else:
            def step(i, c):
                body(i)
                return c
            lax.fori_loop(0, count, step, 0)

    def peers(body):
        def step(k, c):
            body(lax.rem(me + k, n))
            return c
        lax.fori_loop(1, n, step, 0)

    barrier = pltpu.get_barrier_semaphore()
    peers(lambda d: pl.semaphore_signal(barrier, inc=1, device_id={"rows": d}, device_id_type=MESH))
    for k in range(1, nf):
        pl.semaphore_signal(
            barrier, inc=1, device_id={"feat": lax.rem(fid + k, nf)}, device_id_type=MESH
        )

    first = lax.broadcasted_iota(jnp.int32, (8, SL), 0) == 0
    lane = lax.broadcasted_iota(jnp.int32, (1, SL), 1)
    slot = lane // BLK
    for d in range(n):
        live = slot < cnt_ref[d]
        place = jnp.where(live, jnp.where(slot == 0, mol_ref[0, d], mol_ref[1, d]), -1)
        target = jnp.where(slot == 0, rxn_ref[0, d], rxn_ref[1, d]) * BLK + lane % BLK
        tile = jnp.where(live, t_ref[:, d * SL:(d + 1) * SL].astype(F32), 0.0)
        counts = jnp.sum(tile, axis=0, keepdims=True).astype(jnp.int32)
        metas[d] = jnp.where(first, counts, target)
        at = slice((d % gs) * SL, (d % gs + 1) * SL)
        for m in range(MB_DEV):
            here = jnp.where(place == m, tile, 0.0)
            smat[d // gs, m * BLK:(m + 1) * BLK, at] = here.astype(BF16)

    def meta_copy(d, slot):
        return pltpu.make_async_remote_copy(
            src_ref=metas.at[d], dst_ref=metar.at[slot], send_sem=meta_s.at[d],
            recv_sem=meta_r.at[slot], device_id={"rows": d}, device_id_type=MESH,
        )

    ones = jnp.ones((16, MC), BF16)
    vdeg = 1.0 + mm(ones, h_ref[...], NT)
    if groups == 1:
        vdeg = vdeg + mm(jnp.ones((16, gw), BF16), smat[0], NT)
    else:
        vdeg = lax.fori_loop(
            0, groups, lambda g, v: v + mm(jnp.ones((16, gw), BF16), smat[g], NT), vdeg
        )
    vscale = (1.0 / jnp.sqrt(vdeg))[0:1]

    hw = w // PARTS
    parts = [slice(i * hw, (i + 1) * hw) for i in range(PARTS)]

    def a2a(phase, i, d, slot):
        return pltpu.make_async_remote_copy(
            src_ref=sbuf.at[phase, i, d], dst_ref=rbuf.at[phase, i, slot],
            send_sem=a2a_s.at[phase, i, d], recv_sem=a2a_r.at[phase, i, slot],
            device_id={"rows": d}, device_id_type=MESH,
        )

    def produce(phase, i, lhs, mat):
        def part(g):
            p = fold(mm(lhs, mat[g], NN))
            for dd in range(gs):
                sbuf[phase, i, g * gs + dd] = p[:, dd * SL:(dd + 1) * SL]

        each(groups, part)

    def send(phase, i):
        peers(lambda d: a2a(phase, i, d, me).start())
        rbuf[phase, i, me] = sbuf[phase, i, me]

    def collect(phase, i, acc, mat):
        peers(lambda d: a2a(phase, i, d, d).wait_recv())

        def add(g, a):
            got = jnp.concatenate([rbuf[phase, i, g * gs + dd] for dd in range(gs)], axis=1)
            return a + fold(mm(stack(got), mat[g], NT))

        if groups == 1:
            return add(0, acc)
        return lax.fori_loop(0, groups, add, acc)

    lhs = [stack(x_ref[p, :] * vscale) for p in parts]
    for i in range(PARTS):
        produce(0, i, lhs[i], smat)
    edeg = 1.0 + mm(ones, h_ref[...], NN)
    acc = [fold(mm(v, h_ref[...], NN)) for v in lhs]
    pl.semaphore_wait(barrier, n - 1 + nf - 1)
    peers(lambda d: meta_copy(d, me).start())
    metar[me] = metas[me]
    for i in range(PARTS):
        send(0, i)

    peers(lambda d: meta_copy(d, d).wait_recv())

    def fill_e(g, deg):
        for dd in range(gs):
            tgt = metar[g * gs + dd][1:2]
            rows = lax.broadcasted_iota(jnp.int32, (RC, SL), 0)
            emat[g, :, dd * SL:(dd + 1) * SL] = jnp.where(rows == tgt, 1.0, 0.0).astype(BF16)
        cnt = jnp.concatenate([metar[g * gs + dd] for dd in range(gs)], axis=1)
        cnt = jnp.broadcast_to(cnt[0:1], (16, gw)).astype(F32).astype(BF16)
        return deg + mm(cnt, emat[g], NT)

    if groups == 1:
        edeg = fill_e(0, edeg)
    else:
        edeg = lax.fori_loop(0, groups, fill_e, edeg)
    edeg = edeg[0:1]

    lhs = []
    for i in range(PARTS):
        lhs.append(stack(collect(0, i, acc[i], emat) / edeg))
        produce(1, i, lhs[i], emat)
        send(1, i)
    acc = [fold(mm(v, h_ref[...], NT)) for v in lhs]

    def feat_copy(slot, p, i, to):
        ref = gx.at[slot, pl.ds(p * hw, hw)]
        return pltpu.make_async_remote_copy(
            src_ref=ref, dst_ref=ref, send_sem=gx_s.at[i, p], recv_sem=gx_r.at[i, p],
            device_id={"feat": to}, device_id_type=MESH,
        )

    def split_in(f, p):
        hi, lo = split(gx[f, p * hw:(p + 1) * hw, :])
        at = pl.ds(pl.multiple_of(f * w + p * hw, 16), hw)
        xh[at, :] = hi
        xl[at, :] = lo

    relay = nf == 4
    near = fid + 1 - 2 * lax.rem(fid, 2)
    far = lax.rem(fid + 2, nf)
    cross = lax.rem(near + 2, nf)
    sent = []
    for i in range(PARTS):
        gx[fid, parts[i], :] = collect(1, i, acc[i], smat) * vscale
        if relay:
            c = [feat_copy(fid, i, 0, far), feat_copy(fid, i, 1, near)]
        else:
            c = [feat_copy(fid, i, k - 1, lax.rem(fid + k, nf)) for k in range(1, nf)]
        for one in c:
            one.start()
        sent.append(c)
    for i in range(PARTS):
        split_in(fid, i)
    if relay:
        passed = []
        for i in range(PARTS):
            sent[i][0].wait_recv()
            c = feat_copy(far, i, 2, near)
            c.start()
            passed.append(c)
            split_in(far, i)
            sent[i][1].wait_recv()
            split_in(near, i)
        for i in range(PARTS):
            passed[i].wait_recv()
            split_in(cross, i)
        unsent = passed + sum(sent, [])
    else:
        unsent = sum(sent, [])
        for i in range(PARTS):
            for k, c in enumerate(sent[i]):
                c.wait_recv()
                split_in(lax.rem(fid + nf - k - 1, nf), i)

    th, tl = split(tht_ref[...])
    mixed = fold(mm(jnp.concatenate([th, tl], axis=0), xh[...], NN)) + mm(th, xl[...], NN)
    output = jnp.tanh(mixed)
    out_ref[...] = output
    gh, gl = split(cot_ref[...] * (1.0 - output * output))
    partial = fold(mm(jnp.concatenate([gh, gl], axis=0), xh[...], NT)) + mm(gh, xl[...], NT)

    k = w // n
    for d in range(n):
        gsend[d] = partial[d * k:(d + 1) * k]

    def gr(d, slot):
        return pltpu.make_async_remote_copy(
            src_ref=gsend.at[d], dst_ref=grecv.at[slot], send_sem=gr_s.at[d],
            recv_sem=gr_r.at[slot], device_id={"rows": d}, device_id_type=MESH,
        )

    peers(lambda d: gr(d, me).start())
    grecv[me] = gsend[me]
    peers(lambda d: gr(d, d).wait_recv())
    gsum[...] = jnp.sum(grecv[...], axis=0)

    def ga(d, slot):
        return pltpu.make_async_remote_copy(
            src_ref=gsum, dst_ref=gfull.at[slot], send_sem=ga_s.at[d],
            recv_sem=ga_r.at[slot], device_id={"rows": d}, device_id_type=MESH,
        )

    peers(lambda d: ga(d, me).start())
    gfull[me] = gsum[...]
    for c in unsent:
        c.wait_send()
    peers(lambda d: meta_copy(d, d).wait_send())
    peers(lambda d: gr(d, d).wait_send())
    for phase in range(2):
        for i in range(PARTS):
            peers(lambda d: a2a(phase, i, d, d).wait_send())
    peers(lambda d: ga(d, d).wait())
    grad_ref[...] = gfull[...]


def on_device(
    node_feats, theta, cotangent, remote_mol, remote_rxn, remote_count, remote_tiles,
    local_mol, local_rxn, local_tiles,
):
    n = lax.axis_size("rows")
    nf = lax.axis_size("feat")
    gs = min(n, 8)
    groups = n // gs
    gw = gs * SL
    slots = n * CAP
    w, mols = node_feats.shape
    f = w * nf
    vmem = pl.BlockSpec(memory_space=pltpu.VMEM)
    smem = pl.BlockSpec(memory_space=pltpu.SMEM)

    ltiles = local_tiles.reshape(-1, BLK, BLK).astype(BF16)
    ltiles = jnp.concatenate([ltiles, ltiles], axis=2)
    dense = pl.pallas_call(
        local_kernel,
        out_shape=jax.ShapeDtypeStruct((MC, RC), BF16),
        in_specs=[smem, smem, vmem],
        out_specs=vmem,
        compiler_params=pltpu.CompilerParams(vmem_limit_bytes=16 * 2**20),
        name="local_incidence",
    )(local_mol, local_rxn, ltiles)

    rtiles = remote_tiles.reshape(slots, BLK, BLK).astype(BF16)
    rtiles = rtiles.transpose(1, 0, 2).reshape(BLK, slots * BLK)

    dma = pltpu.SemaphoreType.DMA
    out, grad = pl.pallas_call(
        functools.partial(main_kernel, n, nf, gs),
        out_shape=(
            jax.ShapeDtypeStruct((w, mols), F32),
            jax.ShapeDtypeStruct((n, w // n, f), F32),
        ),
        in_specs=[vmem] * 5 + [smem] * 3,
        out_specs=(vmem, vmem),
        scratch_shapes=[
            pltpu.VMEM((nf, w, mols), F32),
            pltpu.VMEM((f, mols), BF16),
            pltpu.VMEM((f, mols), BF16),
            pltpu.VMEM((groups, MC, gw), BF16),
            pltpu.VMEM((groups, RC, gw), BF16),
            pltpu.VMEM((n, 8, SL), jnp.int32),
            pltpu.VMEM((n, 8, SL), jnp.int32),
            pltpu.VMEM((2, PARTS, n, w // PARTS, SL), F32),
            pltpu.VMEM((2, PARTS, n, w // PARTS, SL), F32),
            pltpu.VMEM((n, w // n, f), F32),
            pltpu.VMEM((n, w // n, f), F32),
            pltpu.VMEM((w // n, f), F32),
            pltpu.VMEM((n, w // n, f), F32),
            dma((max(nf - 1, 3), PARTS)), dma((max(nf - 1, 3), PARTS)),
            dma((n,)), dma((n,)),
            dma((2, PARTS, n)), dma((2, PARTS, n)),
            dma((n,)), dma((n,)),
            dma((n,)), dma((n,)),
        ],
        compiler_params=pltpu.CompilerParams(
            collective_id=0, has_side_effects=True,
            vmem_limit_bytes=(28 + n // 2) * 2**20,
        ),
        name="train_step",
    )(node_feats, theta.T, cotangent, dense, rtiles, remote_mol.T, remote_rxn.T, remote_count)
    return out, grad.reshape(w, f).T


def solution(mesh):
    return jax.shard_map(
        on_device,
        mesh=mesh,
        in_specs=(
            P("feat", "rows"),
            P(None, "feat"),
            P("feat", "rows"),
            P("rows", None),
            P("rows", None),
            P("rows"),
            P("rows", None, None),
            P("rows"),
            P("rows"),
            P("rows", None),
        ),
        out_specs=(P("feat", "rows"), P(None, "feat")),
        check_vma=False,
    )
```
